256 devices in a mesh: dp: 32 (over z, x_hi, core), pipe: 8 (over y, x_lo).
Axes of the slice: x: 4 (x_hi: 2, x_lo: 2; x = x_hi * 2 + x_lo), y: 4, z: 8, core: 2. Of those that a mesh axis runs over, the one named last changes fastest.
Arguments:
- tokens: bfloat16 [98304, 4096], P(('dp', 'pipe')), may hold values from -24 to 24
- queries: bfloat16 [98304, 4096], P(('dp', 'pipe')), may hold values from -300 to 300, as said below
- kv_weight: bfloat16 [1024, 4096], P('pipe', 'dp'), may hold values from -0.09375 to 0.09375
- cotangent: bfloat16 [98304, 4096], P(('dp', 'pipe')), may hold values from -0.078125 to 0.078125
Outputs:
- attended: bfloat16 [98304, 4096], P(('dp', 'pipe'))
- kv_grad: float32 [1024, 4096], P('pipe', 'dp')
The draws below stay inside these ranges and needn't reach their ends.
Inputs may be any that keep to these rules, and one draw needn't show every extreme that they name: `queries`: independent normal entries, a scale for each row.
All inputs are finite; a program needn't handle non-finite values.
Results may differ from the reference program's by a relative error of at most 0.02.
The reference program's roundings to bfloat16 on the way (of `key_value`, `probs_half`, `d_scores` and `d_key_value`) count: a program that leaves them out, or rounds other values in their place, can miss the bound.
Values may be sent and summed in bfloat16 or wider, within the bound.
A program may use at most 128 MiB of HBM per device.

```python
import math
import jax
import jax.numpy as jnp
from jax import lax

D = 4096
HEADS = 32
KV_HEADS = 4
HEAD_DIM = 128
TOK_DEV = 384
TOKENS = 98304
KV_WIDTH = 1024


def draw_queries(key, part):
    key = jax.random.fold_in(key, 7)
    key_base, key_scale = jax.random.split(key)
    base_draw = jax.random.normal(key_base, (TOKENS, HEADS * HEAD_DIM), jnp.float32)
    base_draw = jnp.clip(base_draw, -6.0, 6.0)
    row_scale = jnp.exp(jax.random.uniform(key_scale, (TOKENS, 1), jnp.float32, math.log(0.5), math.log(2.0)))
    return (base_draw * row_scale).astype(jnp.bfloat16)


def spiked(entries, own_key, source, target, shards_of, factor):
    owner, partner = [(jnp.arange(entries.shape[position]) // (entries.shape[position] // shards_of)).reshape([-1 if axis == position else 1 for axis in range(entries.ndim)]) for position in (source, target)]
    chosen = jax.random.permutation(own_key, shards_of)[partner]
    strong = (owner == chosen) | (owner == (partner + shards_of // 2) % shards_of)
    return jnp.where(strong, factor * entries, entries)


def levels(rng, shape, cuts, least, top_value):
    level, own = 1.0, jax.random.fold_in(rng, 6)
    for position, blocks in cuts:
        draws = jnp.exp(jax.random.uniform(jax.random.fold_in(own, position), (blocks,), jnp.float32, least / len(cuts), top_value / len(cuts)))
        level = level * jnp.repeat(draws, shape[position] // blocks).reshape([-1 if axis == position else 1 for axis in range(len(shape))])
    return level


def noise(key, shape, spread, bound, cuts=(), held_as=jnp.bfloat16):
    result = jax.random.normal(key, shape, jnp.float32) * spread
    if len(cuts) > 0:
        result = levels(key, shape, cuts, -0.22, 0.18) * result
    return jnp.clip(result, min=-bound, max=bound).astype(held_as)


def bell_draw_with(key, extent, width, reach, cuts, heavy, kind=jnp.bfloat16):
    drawn = width * jax.random.normal(key, extent, jnp.float32)
    if cuts:
        drawn = drawn * levels(key, extent, cuts, -0.22, 0.18)
    return jnp.clip(spiked(drawn, jax.random.fold_in(key, 3), *heavy), -reach, reach).astype(kind)


def setup_inputs(seed: int = 0) -> dict:
    splits = jax.random.split(jax.random.key(seed), 5)
    return {
        "tokens": bell_draw_with(splits[0], (TOKENS, D), 1.0, 24.0, ((0, 256),), (0, 1, 256, 6.0)),
        "queries": draw_queries(jax.random.fold_in(splits[4], 71), 0),
        "kv_weight": noise(splits[2], (KV_WIDTH, D), D ** -0.5, 0.09375, ((0, 8), (1, 32))),
        "cotangent": noise(splits[3], (TOKENS, HEADS * HEAD_DIM), (4.0 / TOKENS ** 0.5), 0.078125, ((0, 256),)),
    }


def attention(query_rows, key_value):
    seq_len = query_rows.shape[0]
    groups = HEADS // KV_HEADS
    scale_factor = 1.0 / (HEAD_DIM ** 0.5)
    query_heads = query_rows.reshape(seq_len, KV_HEADS, groups, HEAD_DIM)
    key_heads = key_value[:, :KV_HEADS * HEAD_DIM].reshape(seq_len, KV_HEADS, HEAD_DIM)
    value_heads = key_value[:, KV_HEADS * HEAD_DIM:].reshape(seq_len, KV_HEADS, HEAD_DIM)
    scores = jnp.einsum("sngd,tnd->ngst", query_heads, key_heads, preferred_element_type=jnp.float32) * scale_factor
    causal = jnp.arange(seq_len)[:, None] >= jnp.arange(seq_len)[None, :]
    scores = jnp.where(causal, scores, jnp.float32(-1e30))
    row_max = jnp.max(scores, axis=-1, keepdims=True)
    expsum = jnp.exp(scores - row_max)
    probs_fp = expsum / jnp.sum(expsum, axis=-1, keepdims=True)
    probs_half = probs_fp.astype(jnp.bfloat16)
    output = jnp.einsum("ngst,tnd->sngd", probs_half, value_heads, preferred_element_type=jnp.float32)
    attended = output.reshape(seq_len, HEADS * HEAD_DIM).astype(jnp.bfloat16)
    return attended, probs_fp, probs_half, query_heads, value_heads


def attention_back(cotangent, probs_fp, probs_half, query_heads, value_heads):
    seq_len = cotangent.shape[0]
    groups = HEADS // KV_HEADS
    scale_factor = 1.0 / (HEAD_DIM ** 0.5)
    grad_heads = cotangent.reshape(seq_len, KV_HEADS, groups, HEAD_DIM)
    d_values = jnp.einsum("ngst,sngd->tnd", probs_half, grad_heads, preferred_element_type=jnp.float32)
    d_probs = jnp.einsum("sngd,tnd->ngst", grad_heads, value_heads, preferred_element_type=jnp.float32)
    inner = jnp.sum(probs_fp * d_probs, axis=-1, keepdims=True)
    d_scores = (probs_fp * (d_probs - inner) * scale_factor).astype(jnp.bfloat16)
    d_keys = jnp.einsum("ngst,sngd->tnd", d_scores, query_heads, preferred_element_type=jnp.float32)
    return jnp.concatenate([d_keys.reshape(seq_len, -1), d_values.reshape(seq_len, -1)], axis=1).astype(jnp.bfloat16)


def one_sequence(pieces):
    token_rows, query_rows, grad_rows, kv_weight = pieces
    key_value = jnp.einsum("sd,rd->sr", token_rows, kv_weight, preferred_element_type=jnp.float32).astype(jnp.bfloat16)
    attended, probs_fp, probs_half, query_heads, value_heads = attention(query_rows, key_value)
    d_key_value = attention_back(grad_rows, probs_fp, probs_half, query_heads, value_heads)
    return attended, d_key_value


def reference(tokens, queries, kv_weight, cotangent):
    count = TOKENS // TOK_DEV
    token_seqs = tokens.reshape(count, TOK_DEV, D)
    query_seqs = queries.reshape(count, TOK_DEV, HEADS * HEAD_DIM)
    grad_seqs = cotangent.reshape(count, TOK_DEV, HEADS * HEAD_DIM)

    def step(pieces):
        return one_sequence((pieces[0], pieces[1], pieces[2], kv_weight))

    attended, d_key_value = lax.map(step, (token_seqs, query_seqs, grad_seqs))
    attended = attended.reshape(TOKENS, HEADS * HEAD_DIM)
    d_key_value = d_key_value.reshape(TOKENS, KV_WIDTH)
    kv_grad = jnp.einsum("sr,sd->rd", d_key_value, tokens, preferred_element_type=jnp.float32)
    return attended, kv_grad
```

```python
import functools
import math

import jax
import jax.numpy as jnp
from jax import lax
from jax.experimental import pallas as pl
from jax.experimental.pallas import tpu as pltpu
from jax.sharding import PartitionSpec as P

SEQ = 384
WIDTH = 4096
HALF = 2048
KV_HEADS = 4
PAIRS = 4
HEAD = 128
SCALE = 1.0 / math.sqrt(HEAD)
LOG2E = math.log2(math.e)
MESH = pl.DeviceIdType.MESH
F32 = jnp.float32
BF16 = jnp.bfloat16
NT = (((1,), (1,)), ((), ()))


def place(x, y, z, c):
    return (z * 4 + (x // 2) * 2 + c, y * 2 + x % 2)


def kernel(
    tokens, queries, weight, cotangent, attended, kv_grad,
    tok, qry, cot, out, gathered, head_weight, part_send, part_own, part_recv,
    kv, d_kv, d_kv_t, acc, u_half, u_full, v_half, v_full, z_recv, done, owned,
    load_sem, tok_sem, ag_send, ag_recv, part_ssem, part_rsem, dkv_ssem, dkv_rsem,
    u_ssem, u_rsem, v_ssem, v_rsem, z_ssem, z_rsem, own_ssem, own_rsem, out_sem,
):
    dp, pipe = lax.axis_index("dp"), lax.axis_index("pipe")
    c, x, y, z = dp % 2, 2 * ((dp // 2) % 2) + pipe % 2, pipe // 2, dp // 4
    u, v = x + c * (y - x), y + c * (x - y)

    def uv(a, b):
        return place(a + c * (b - a), b + c * (a - b), z, c)

    def u_dev(step):
        return uv((u + step) % 4, v)

    def v_dev(step):
        return uv(u, (v + step) % 4)

    def z_dev(step):
        return place(x, y, (z + step) % 8, c)

    sibling = place(x, y, z, 1 - c)
    quad = 2 * (y % 2) + x % 2

    def remote(src, dst, ssem, rsem, device):
        return pltpu.make_async_remote_copy(
            src_ref=src, dst_ref=dst, send_sem=ssem, recv_sem=rsem,
            device_id=device, device_id_type=MESH,
        )

    own_weight = pltpu.make_async_copy(weight, gathered.at[u, v, z], load_sem.at[0])
    own_weight.start()

    def load_tokens(k, _):
        pltpu.make_async_copy(
            tokens.at[:, pl.ds(pl.multiple_of((2 * k + c) * 128, 128), 128)],
            tok.at[pl.ds(pl.multiple_of(c * SEQ, SEQ), SEQ), pl.ds(pl.multiple_of(k * 128, 128), 128)],
            load_sem.at[1],
        ).start()
        return 0

    lax.fori_loop(0, 16, load_tokens, 0)
    all_queries = pltpu.make_async_copy(queries, qry, load_sem.at[2])
    all_cot = pltpu.make_async_copy(cotangent, cot, load_sem.at[3])
    all_queries.start()
    all_cot.start()

    barrier = pltpu.get_barrier_semaphore()
    peers = [u_dev(1), u_dev(-1 + 4), v_dev(1), v_dev(-1 + 4), sibling]
    peers += [z_dev(k) for k in range(1, 8)]
    peers += [place(x + 1 - 2 * (x % 2), y + 1 - 2 * (y % 2), z, c)]
    for peer in peers:
        pl.semaphore_signal(barrier, inc=1, device_id=peer, device_id_type=MESH)
    pl.semaphore_wait(barrier, len(peers))

    own_weight.wait()
    mine = gathered.at[u, v, z]
    for k in range(1, 8):
        remote(mine, mine, ag_send.at[k], ag_recv.at[k], z_dev(k)).start()

    my_rows = pl.ds(pl.multiple_of(c * SEQ, SEQ), SEQ)
    sib_rows = pl.ds(pl.multiple_of((1 - c) * SEQ, SEQ), SEQ)

    def send_tokens(k, _):
        remote(
            tokens.at[:, pl.ds(pl.multiple_of((2 * k + 1 - c) * 128, 128), 128)],
            tok.at[my_rows, pl.ds(pl.multiple_of(k * 128, 128), 128)],
            tok_sem.at[0], tok_sem.at[1], sibling,
        ).start()
        return 0

    lax.fori_loop(0, 16, send_tokens, 0)

    for k in range(1, 8):
        here = gathered.at[u, v, (z - k + 8) % 8]
        remote(mine, here, ag_send.at[k], ag_recv.at[k], z_dev(k)).wait_recv()

    def v_first(step, sem):
        row = gathered.at[u, v]
        return remote(row, row, ag_send.at[sem], ag_recv.at[sem], v_dev(step))

    def v_second(step, sem):
        row = gathered.at[u, (v - step + 4) % 4, pl.ds(0 if step == 1 else 4, 4)]
        return remote(row, row, ag_send.at[sem], ag_recv.at[sem], v_dev((step + 4) % 4))

    def u_first(step, rel, sem):
        row = gathered.at[u, (v + rel + 4) % 4]
        return remote(row, row, ag_send.at[sem], ag_recv.at[sem], u_dev((step + 4) % 4))

    def u_second(step, rel, sem):
        row = gathered.at[(u - step + 4) % 4, (v + rel + 4) % 4, pl.ds(0 if step == 1 else 4, 4)]
        return remote(row, row, ag_send.at[sem], ag_recv.at[sem], u_dev((step + 4) % 4))

    rels = (0, -1, 1, 2)
    va = [v_first(1, 8), v_first(3, 9)]
    vb = [v_second(1, 10), v_second(-1, 11)]
    ua = {r: [u_first(1, r, 12 + 2 * i), u_first(-1, r, 13 + 2 * i)] for i, r in enumerate(rels)}
    ub = {r: [u_second(1, r, 20 + 2 * i), u_second(-1, r, 21 + 2 * i)] for i, r in enumerate(rels)}

    def start(copies):
        for copy in copies:
            copy.start()

    def landed(copies):
        for copy in copies:
            copy.wait_recv()

    def sent(copies):
        for copy in copies:
            copy.wait_send()

    start(va)
    start(ua[0])
    landed(va)
    start(vb)
    start(ua[-1])
    start(ua[1])
    landed(ua[0])
    start(ub[0])
    landed(vb)
    start(ua[2])
    landed(ua[-1])
    start(ub[-1])
    landed(ua[1])
    start(ub[1])
    landed(ua[2])
    start(ub[2])
    own_tok = pltpu.make_async_copy(tok.at[my_rows], tok.at[my_rows], load_sem.at[1])
    own_tok.wait()
    tok_all = remote(tok.at[my_rows], tok.at[sib_rows], tok_sem.at[0], tok_sem.at[1], sibling)
    tok_all.wait_recv()
    for r in rels:
        landed(ub[r])

    def part_copy(n):
        return remote(part_send.at[n], part_recv.at[n], part_ssem.at[n], part_rsem.at[n], sibling)

    def project(n):
        for kind in range(2):
            for x_hi in range(2):
                wx, wy = 2 * x_hi + n % 2, n // 2 + 2 * kind
                wu, wv = wx + c * (wy - wx), wy + c * (wx - wy)
                for wz in range(8):
                    k = wz * 2 + x_hi
                    head_weight[kind * 128:(kind + 1) * 128, k * 128:(k + 1) * 128] = gathered[wu, wv, wz]
        part_send[n] = lax.dot_general(tok[sib_rows, :], head_weight[...], NT, preferred_element_type=F32)
        part_copy(n).start()
        part_own[n] = lax.dot_general(tok[my_rows, :], head_weight[...], NT, preferred_element_type=F32)

    def attend(n, p):
        base = pl.multiple_of((n * PAIRS + p) * 256, 256)
        for j in range(3):
            rows, span = slice(j * 128, (j + 1) * 128), (j + 1) * 128
            q = qry[rows, pl.ds(base, 256)]
            g = cot[rows, pl.ds(base, 256)]
            q = jnp.concatenate([q[:, :128], q[:, 128:]], axis=0)
            g = jnp.concatenate([g[:, :128], g[:, 128:]], axis=0)
            keys, values = kv[:span, :128], kv[:span, 128:]
            scores = lax.dot_general(keys, q, NT, preferred_element_type=F32) * SCALE
            at_key = lax.broadcasted_iota(jnp.int32, (128, 256), 0)
            at_query = lax.broadcasted_iota(jnp.int32, (128, 256), 1) % 128
            diagonal = jnp.where(at_key <= at_query, scores[j * 128:], -1e30)
            scores = diagonal if j == 0 else jnp.concatenate([scores[: j * 128], diagonal], axis=0)
            top = jnp.max(scores, axis=0, keepdims=True)
            grown = jnp.exp2((scores - top) * LOG2E)
            probs = grown * (1.0 / jnp.sum(grown, axis=0, keepdims=True))
            probs_half = probs.astype(BF16)
            seen = lax.dot_general(
                values, probs_half, (((0,), (0,)), ((), ())), preferred_element_type=F32
            ).astype(BF16)
            out[rows, pl.ds(base, 128)] = seen[:, :128].T
            out[rows, pl.ds(base + 128, 128)] = seen[:, 128:].T
            d_probs = lax.dot_general(values, g, NT, preferred_element_type=F32)
            inner = jnp.sum(probs * d_probs, axis=0, keepdims=True)
            d_scores = (probs * (d_probs - inner) * SCALE).astype(BF16)
            d_kv[:span, :128] += jnp.dot(d_scores, q, preferred_element_type=F32)
            d_kv[:span, 128:] += jnp.dot(probs_half, g, preferred_element_type=F32)

    def dkv_copy(n):
        here = d_kv_t.at[n, :, my_rows]
        return remote(here, here, dkv_ssem.at[n], dkv_rsem.at[n], sibling)

    def dkv_landed(n):
        here = d_kv_t.at[n, :, sib_rows]
        remote(here, here, dkv_ssem.at[n], dkv_rsem.at[n], sibling).wait_recv()

    def gradient(n):
        lhs = d_kv_t[n]

        @pl.loop(0, 8)
        def _(gz):
            cols = pl.ds(pl.multiple_of(gz * 256, 256), 256)
            block = jnp.dot(lhs, tok[:, cols], preferred_element_type=F32)
            for kind in range(2):
                for q in range(4):
                    for x_hi in range(2):
                        gx, gy = 2 * x_hi + q % 2, 2 * kind + q // 2
                        gu, gv = gx + c * (gy - gx), gy + c * (gx - gy)
                        row = kind * 128 + q * 32
                        acc[n, gu, gv, gz] = block[row:row + 32, x_hi * 128:(x_hi + 1) * 128]

    def u_halves(n):
        far = (u + 2) % 4
        return [
            remote(acc.at[n, far, :, pl.ds(4 * i, 4)], u_half.at[n, i], u_ssem.at[n, i], u_rsem.at[n, i], u_dev(1 + 2 * i))
            for i in range(2)
        ]

    def u_fulls(n):
        return [
            remote(acc.at[n, (u + 1 + 2 * i) % 4], u_full.at[n, i], u_ssem.at[n, 2 + i], u_rsem.at[n, 2 + i], u_dev(1 + 2 * i))
            for i in range(2)
        ]

    def v_halves(n):
        far = (v + 2) % 4
        return [
            remote(acc.at[n, u, far, pl.ds(4 * i, 4)], v_half.at[n, i], v_ssem.at[n, i], v_rsem.at[n, i], v_dev(1 + 2 * i))
            for i in range(2)
        ]

    def v_fulls(n):
        return [
            remote(acc.at[n, u, (v + 1 + 2 * i) % 4], v_full.at[n, i], v_ssem.at[n, 2 + i], v_rsem.at[n, 2 + i], v_dev(1 + 2 * i))
            for i in range(2)
        ]

    def z_all(n):
        return [
            remote(acc.at[n, u, v, (z + k) % 8], z_recv.at[n, k - 1], z_ssem.at[n, k - 1], z_rsem.at[n, k - 1], z_dev(k))
            for k in range(1, 8)
        ]

    def to_owner(n):
        there = place(x - x % 2 + n % 2, y - y % 2 + n // 2, z, c)
        return remote(done.at[n], owned.at[quad], own_ssem.at[n], own_rsem.at[quad], there)

    def stage0(n):
        start(u_halves(n))

    def stage1(n):
        copies = u_halves(n)
        landed(copies)
        for i in range(2):
            near = (u + 1 + 2 * i) % 4
            for b in range(4):
                acc[n, near, b, pl.ds(4 * i, 4)] += u_half[n, i, b]
        start(u_fulls(n))
        sent(copies)

    def stage2(n):
        copies = u_fulls(n)
        landed(copies)
        for b in range(4):
            acc[n, u, b] += u_full[n, 0, b] + u_full[n, 1, b]
        start(v_halves(n))
        sent(copies)

    def stage3(n):
        copies = v_halves(n)
        landed(copies)
        for i in range(2):
            near = (v + 1 + 2 * i) % 4
            acc[n, u, near, pl.ds(4 * i, 4)] += v_half[n, i]
        start(v_fulls(n))
        sent(copies)

    def stage4(n):
        copies = v_fulls(n)
        landed(copies)
        acc[n, u, v] += v_full[n, 0] + v_full[n, 1]
        start(z_all(n))
        sent(copies)

    def stage5(n):
        copies = z_all(n)
        landed(copies)
        total = acc[n, u, v, z]
        for k in range(7):
            total = total + z_recv[n, k]

        @pl.when(quad == n)
        def _():
            owned[quad] = total

        @pl.when(quad != n)
        def _():
            done[n] = total
            to_owner(n).start()

        sent(copies)

    def out_copy(n):
        cols = pl.ds(pl.multiple_of(n * 1024, 1024), 1024)
        return pltpu.make_async_copy(out.at[:, cols], attended.at[:, cols], out_sem.at[n])

    project(0)
    project(1)
    project(2)
    project(3)
    all_queries.wait()
    all_cot.wait()

    def head(n, _):
        part_copy(n).wait_recv()
        kv[...] = (part_own[n] + part_recv[n]).astype(BF16)
        d_kv[...] = jnp.zeros_like(d_kv)
        attend(n, 0)
        pl.when(n >= 2)(lambda: stage3(n - 2))
        attend(n, 1)
        pl.when(n >= 1)(lambda: stage1(n - 1))
        attend(n, 2)
        pl.when(n >= 2)(lambda: stage4(n - 2))
        attend(n, 3)
        out_copy(n).start()
        d_kv_t[n, :, my_rows] = d_kv[...].astype(BF16).T
        dkv_copy(n).start()
        dkv_landed(n)
        gradient(n)
        stage0(n)
        pl.when(n >= 1)(lambda: stage2(n - 1))
        pl.when(n >= 2)(lambda: stage5(n - 2))
        return 0

    lax.fori_loop(0, KV_HEADS, head, 0)
    stage3(2)
    stage1(3)
    stage4(2)
    stage2(3)
    stage5(2)
    stage3(3)
    stage4(3)
    stage5(3)

    for q in range(4):

        @pl.when(quad != q)
        def _():
            to_owner(q).wait_send()
            remote(done.at[q], owned.at[q], own_ssem.at[q], own_rsem.at[q], sibling).wait_recv()

    for q in range(4):
        kv_grad[q * 32:(q + 1) * 32, :] = owned[q]
    for k in range(1, 8):
        remote(mine, mine, ag_send.at[k], ag_recv.at[k], z_dev(k)).wait_send()
    sent(va)
    sent(vb)
    for r in rels:
        sent(ua[r])
        sent(ub[r])
    tok_all.wait_send()
    for n in range(KV_HEADS):
        part_copy(n).wait_send()
        dkv_copy(n).wait_send()
        out_copy(n).wait()


def on_device(tokens, queries, weight, cotangent):
    anywhere = pl.BlockSpec(memory_space=pl.ANY)
    vmem = pltpu.VMEM
    dma = pltpu.SemaphoreType.DMA
    return pl.pallas_call(
        kernel,
        out_shape=(
            jax.ShapeDtypeStruct((SEQ, WIDTH), BF16),
            jax.ShapeDtypeStruct((128, 128), F32),
        ),
        in_specs=[anywhere] * 4,
        out_specs=(anywhere, pl.BlockSpec(memory_space=vmem)),
        scratch_shapes=[
            vmem((2 * SEQ, HALF), BF16),
            vmem((SEQ, WIDTH), BF16),
            vmem((SEQ, WIDTH), BF16),
            vmem((SEQ, WIDTH), BF16),
            vmem((4, 4, 8, 128, 128), BF16),
            vmem((256, HALF), BF16),
            vmem((4, SEQ, 256), F32),
            vmem((4, SEQ, 256), F32),
            vmem((4, SEQ, 256), F32),
            vmem((SEQ, 256), BF16),
            vmem((SEQ, 256), F32),
            vmem((4, 256, 2 * SEQ), BF16),
            vmem((4, 4, 4, 8, 32, 128), F32),
            vmem((4, 2, 4, 4, 32, 128), F32),
            vmem((4, 2, 4, 8, 32, 128), F32),
            vmem((4, 2, 4, 32, 128), F32),
            vmem((4, 2, 8, 32, 128), F32),
            vmem((4, 7, 32, 128), F32),
            vmem((4, 32, 128), F32),
            vmem((4, 32, 128), F32),
            dma((4,)),
            dma((2,)),
            dma((28,)),
            dma((28,)),
            dma((4,)),
            dma((4,)),
            dma((4,)),
            dma((4,)),
            dma((4, 4)),
            dma((4, 4)),
            dma((4, 4)),
            dma((4, 4)),
            dma((4, 7)),
            dma((4, 7)),
            dma((4,)),
            dma((4,)),
            dma((4,)),
        ],
        compiler_params=pltpu.CompilerParams(
            collective_id=0, has_side_effects=True, vmem_limit_bytes=56 * 2**20
        ),
        cost_estimate=pl.CostEstimate(flops=12 * 10**9, bytes_accessed=16 * 2**20, transcendentals=4 * 10**6),
    )(tokens, queries, weight, cotangent)


def solution(mesh):
    placed = (
        P(("dp", "pipe"), None),
        P(("dp", "pipe"), None),
        P("pipe", "dp"),
        P(("dp", "pipe"), None),
    )
    return jax.shard_map(
        on_device,
        mesh=mesh,
        in_specs=placed,
        out_specs=(P(("dp", "pipe"), None), P("pipe", "dp")),
        check_vma=False,
    )
```

```python
import functools
import math

import jax
import jax.numpy as jnp
from jax import lax
from jax.experimental import pallas as pl
from jax.experimental.pallas import tpu as pltpu
from jax.sharding import PartitionSpec as P

SEQ = 384
WIDTH = 4096
HALF = 2048
KV_HEADS = 4
HEAD = 128
SCALE = 1.0 / math.sqrt(HEAD)
LOG2E = math.log2(math.e)
MESH = pl.DeviceIdType.MESH
F32 = jnp.float32
BF16 = jnp.bfloat16
MAIN = 96
NT = (((1,), (1,)), ((), ()))


def place(x, y, z, c):
    return (z * 4 + (x // 2) * 2 + c, y * 2 + x % 2)


def kernel(
    tokens, queries, weight, cotangent, attended, kv_grad,
    tok, far_tok, qry, cot, out, gathered, gathered_z, head_weight, part_send, part_own, part_recv,
    kv, d_kv, d_kv_t, far_kv_t, acc, u_half, u_full, v_recv, z_recv, done, owned,
    load_sem, tok_sem, ag_send, ag_recv, zg_send, zg_recv, part_ssem, part_rsem, dkv_ssem, dkv_rsem, far_send, far_recv,
    u_ssem, u_rsem, v_ssem, v_rsem, z_ssem, z_rsem, own_ssem, own_rsem, out_sem,
):
    dp, pipe = lax.axis_index("dp"), lax.axis_index("pipe")
    c, x, y, z = dp % 2, 2 * ((dp // 2) % 2) + pipe % 2, pipe // 2, dp // 4
    u, v = x + c * (y - x), y + c * (x - y)

    def uv(a, b):
        return place(a + c * (b - a), b + c * (a - b), z, c)

    def u_dev(step):
        return uv((u + step) % 4, v)

    def v_dev(step):
        return uv(u, (v + step) % 4)

    def z_dev(step):
        return place(x, y, (z + step) % 8, c)

    sibling = place(x, y, z, 1 - c)
    z_odd, z_half = z % 2, z // 2
    partner = [place(x, y, z + 1 - 2 * z_odd, c), place(x, y, z + 1 - 2 * z_odd, 1 - c)]
    quad = 2 * (y % 2) + x % 2

    def remote(src, dst, ssem, rsem, device):
        return pltpu.make_async_remote_copy(
            src_ref=src, dst_ref=dst, send_sem=ssem, recv_sem=rsem,
            device_id=device, device_id_type=MESH,
        )

    own_weight = pltpu.make_async_copy(weight.at[pl.ds(0, MAIN)], gathered.at[u, v, z], load_sem.at[0])
    own_rest = pltpu.make_async_copy(weight.at[pl.ds(MAIN, 128 - MAIN)], gathered_z.at[z, u, v], load_sem.at[4])
    own_weight.start()
    own_rest.start()

    def load_tokens(k, _):
        pltpu.make_async_copy(
            tokens.at[:, pl.ds(pl.multiple_of((2 * k + c) * 128, 128), 128)],
            tok.at[pl.ds(pl.multiple_of(c * SEQ, SEQ), SEQ), pl.ds(pl.multiple_of(k * 128, 128), 128)],
            load_sem.at[1],
        ).start()
        return 0

    lax.fori_loop(0, 16, load_tokens, 0)
    all_queries = pltpu.make_async_copy(queries, qry, load_sem.at[2])
    all_cot = pltpu.make_async_copy(cotangent, cot, load_sem.at[3])
    all_queries.start()
    all_cot.start()

    barrier = pltpu.get_barrier_semaphore()
    peers = [u_dev(k) for k in range(1, 4)] + [v_dev(k) for k in range(1, 4)] + [sibling]
    peers += [z_dev(k) for k in range(1, 8)]
    peers += [place(x + 1 - 2 * (x % 2), y + 1 - 2 * (y % 2), z, c), partner[1]]
    for peer in peers:
        pl.semaphore_signal(barrier, inc=1, device_id=peer, device_id_type=MESH)
    pl.semaphore_wait(barrier, len(peers))

    own_weight.wait()
    mine = gathered.at[u, v, z]
    for k in range(1, 8):
        remote(mine, mine, ag_send.at[k], ag_recv.at[k], z_dev(k)).start()

    own_rest.wait()

    def zv(k):
        here = gathered_z.at[z, u, v]
        return remote(here, here, zg_send.at[k], zg_recv.at[k], v_dev(k))

    def zu(k):
        here = gathered_z.at[z, u]
        return remote(here, here, zg_send.at[3 + k], zg_recv.at[3 + k], u_dev(k))

    def zz(hop, way):
        here = gathered_z.at[(z - way * hop + 8) % 8]
        if hop == 3:
            here = here.at[pl.ds(0 if way == 1 else 2, 2)]
        sem = 7 + 2 * hop + (way == -1)
        return remote(here, here, zg_send.at[sem], zg_recv.at[sem], z_dev(8 + way))

    zvs = [zv(k) for k in range(1, 4)]
    zus = [zu(k) for k in range(1, 4)]
    zzs = [[zz(hop, 1), zz(hop, -1)] for hop in range(4)]
    for copy in zvs:
        copy.start()

    my_rows = pl.ds(pl.multiple_of(c * SEQ, SEQ), SEQ)
    sib_rows = pl.ds(pl.multiple_of((1 - c) * SEQ, SEQ), SEQ)

    def send_tokens(k, _):
        remote(
            tokens.at[:, pl.ds(pl.multiple_of((2 * k + 1 - c) * 128, 128), 128)],
            tok.at[my_rows, pl.ds(pl.multiple_of(k * 128, 128), 128)],
            tok_sem.at[0], tok_sem.at[1], sibling,
        ).start()
        return 0

    lax.fori_loop(0, 16, send_tokens, 0)

    def v_first(step, sem):
        row = gathered.at[u, v]
        return remote(row, row, ag_send.at[sem], ag_recv.at[sem], v_dev(step))

    def v_second(step, sem):
        row = gathered.at[u, (v - step + 4) % 4, pl.ds(0 if step == 1 else 4, 4)]
        return remote(row, row, ag_send.at[sem], ag_recv.at[sem], v_dev((step + 4) % 4))

    def u_first(step, rel, sem):
        row = gathered.at[u, (v + rel + 4) % 4]
        return remote(row, row, ag_send.at[sem], ag_recv.at[sem], u_dev((step + 4) % 4))

    def u_second(step, rel, sem):
        row = gathered.at[(u - step + 4) % 4, (v + rel + 4) % 4, pl.ds(0 if step == 1 else 4, 4)]
        return remote(row, row, ag_send.at[sem], ag_recv.at[sem], u_dev((step + 4) % 4))

    rels = (0, -1, 1, 2)
    va = [v_first(1, 8), v_first(3, 9)]
    vb = [v_second(1, 10), v_second(-1, 11)]
    ua = {r: [u_first(1, r, 12 + 2 * i), u_first(-1, r, 13 + 2 * i)] for i, r in enumerate(rels)}
    ub = {r: [u_second(1, r, 20 + 2 * i), u_second(-1, r, 21 + 2 * i)] for i, r in enumerate(rels)}

    def start(copies):
        for copy in copies:
            copy.start()

    def landed(copies):
        for copy in copies:
            copy.wait_recv()

    def sent(copies):
        for copy in copies:
            copy.wait_send()

    def share(first, last):
        for i in range(first, last):
            core, block = i // 8, i % 8
            target = c if core == 0 else 1 - c
            column = (2 * (block // 2) + 1 - z_odd) * 4 + 2 * (block % 2) + target
            remote(
                tokens.at[:, pl.ds(pl.multiple_of(column * 128, 128), 128)],
                far_tok.at[my_rows, pl.ds(block * 128, 128)],
                far_send.at[core], far_recv.at[core], partner[core],
            ).start()

    landed(zvs)
    start(zus)
    for k in range(1, 8):
        here = gathered.at[u, v, (z - k + 8) % 8]
        remote(mine, here, ag_send.at[k], ag_recv.at[k], z_dev(k)).wait_recv()
    start(va)
    start(ua[0])
    landed(zus)
    start(zzs[0])
    share(0, 2)
    landed(va)
    start(vb)
    start(ua[-1])
    start(ua[1])
    landed(zzs[0])
    start(zzs[1])
    share(2, 4)
    landed(ua[0])
    start(ub[0])
    landed(vb)
    start(ua[2])
    landed(zzs[1])
    start(zzs[2])
    share(4, 6)
    landed(ua[-1])
    start(ub[-1])
    landed(ua[1])
    start(ub[1])
    landed(zzs[2])
    start(zzs[3])
    share(6, 16)
    landed(ua[2])
    start(ub[2])
    own_tok = pltpu.make_async_copy(tok.at[my_rows], tok.at[my_rows], load_sem.at[1])
    own_tok.wait()
    tok_all = remote(tok.at[my_rows], tok.at[sib_rows], tok_sem.at[0], tok_sem.at[1], sibling)
    tok_all.wait_recv()
    for r in rels:
        landed(ub[r])
    landed(zzs[3])

    def part_copy(n):
        return remote(part_send.at[n], part_recv.at[n], part_ssem.at[n], part_rsem.at[n], sibling)

    def project(n):
        for kind in range(2):
            for x_hi in range(2):
                wx, wy = 2 * x_hi + n % 2, n // 2 + 2 * kind
                wu, wv = wx + c * (wy - wx), wy + c * (wx - wy)
                for wz in range(8):
                    k = wz * 2 + x_hi
                    cols, row = slice(k * 128, (k + 1) * 128), kind * 128
                    head_weight[row:row + MAIN, cols] = gathered[wu, wv, wz]
                    head_weight[row + MAIN:row + 128, cols] = gathered_z[wz, wu, wv]
        part_send[n] = lax.dot_general(tok[sib_rows, :], head_weight[...], NT, preferred_element_type=F32)
        part_copy(n).start()
        part_own[n] = lax.dot_general(tok[my_rows, :], head_weight[...], NT, preferred_element_type=F32)

    def attend(n, p):
        base = pl.multiple_of((n * 2 + p) * 512, 512)
        at_key = lax.broadcasted_iota(jnp.int32, (128, 512), 0)
        at_query = lax.broadcasted_iota(jnp.int32, (128, 512), 1) % 128

        def heads(ref, j):
            block = ref[j * 128:(j + 1) * 128, pl.ds(base, 512)]
            return jnp.concatenate([block[:, h * 128:(h + 1) * 128] for h in range(4)], axis=0)

        def products(j):
            q, g, span = heads(qry, j), heads(cot, j), (j + 1) * 128
            scores = lax.dot_general(kv[:span, :128], q, NT, preferred_element_type=F32)
            d_probs = lax.dot_general(kv[:span, 128:], g, NT, preferred_element_type=F32)
            return q, g, scores, d_probs

        def softmax(j, scores, d_probs):
            diagonal = jnp.where(at_key <= at_query, scores[j * 128:], -1e30)
            scores = diagonal if j == 0 else jnp.concatenate([scores[: j * 128], diagonal], axis=0)
            top = jnp.max(scores, axis=0, keepdims=True)
            grown = jnp.exp2((scores - top) * (SCALE * LOG2E))
            share_of = 1.0 / jnp.sum(grown, axis=0, keepdims=True)
            weighed = grown * d_probs
            inner = jnp.sum(weighed, axis=0, keepdims=True) * share_of
            d_scores = (weighed - grown * inner) * (share_of * SCALE)
            return (grown * share_of).astype(BF16), d_scores.astype(BF16)

        blocks = [products(j) for j in range(3)]
        halves = [softmax(j, blocks[j][2], blocks[j][3]) for j in range(3)]
        d_keys, d_values = [], []
        for j in range(3):
            q, g = blocks[j][:2]
            probs_half, d_scores = halves[j]
            seen = lax.dot_general(
                kv[: (j + 1) * 128, 128:], probs_half, (((0,), (0,)), ((), ())), preferred_element_type=F32
            ).astype(BF16)
            for h in range(4):
                out[j * 128:(j + 1) * 128, pl.ds(base + h * 128, 128)] = seen[:, h * 128:(h + 1) * 128].T
            d_keys.append(jnp.dot(d_scores, q, preferred_element_type=F32))
            d_values.append(jnp.dot(probs_half, g, preferred_element_type=F32))
        for t in range(3):
            rows = slice(t * 128, (t + 1) * 128)
            d_kv[rows, :128] += sum(d_keys[j][rows] for j in range(t, 3))
            d_kv[rows, 128:] += sum(d_values[j][rows] for j in range(t, 3))

    def dkv_copies(n):
        here, there = d_kv_t.at[n, :, my_rows], far_kv_t.at[n, :, my_rows]
        return [
            remote(here, here, dkv_ssem.at[n, 0], dkv_rsem.at[n, 0], sibling),
            remote(here, there, dkv_ssem.at[n, 1], dkv_rsem.at[n, 1], partner[0]),
            remote(there, there, dkv_ssem.at[n, 2], dkv_rsem.at[n, 2], sibling),
        ]

    def forward(n):
        copies = dkv_copies(n)
        copies[1].wait_recv()
        copies[2].start()

    def gradient(n):
        copies = dkv_copies(n)
        copies[0].wait_recv()
        if n == 0:
            for core in range(2):
                rows = far_tok.at[my_rows if core == 0 else sib_rows]
                remote(rows, rows, far_send.at[core], far_recv.at[core], partner[core]).wait_recv()
        copies[2].wait_recv()
        near, far = d_kv_t[n], far_kv_t[n]

        @pl.loop(0, 4)
        def _(gz):
            cols = pl.ds(pl.multiple_of((2 * gz + z_odd) * 256, 256), 256)
            far_cols = pl.ds(pl.multiple_of(gz * 256, 256), 256)
            block = jnp.dot(near, tok[:, cols], preferred_element_type=F32)
            block += jnp.dot(far, far_tok[:, far_cols], preferred_element_type=F32)
            for kind in range(2):
                for q in range(4):
                    for x_hi in range(2):
                        gx, gy = 2 * x_hi + q % 2, 2 * kind + q // 2
                        gu, gv = gx + c * (gy - gx), gy + c * (gx - gy)
                        row = kind * 128 + q * 32
                        acc[n, gu, gv, gz] = block[row:row + 32, x_hi * 128:(x_hi + 1) * 128]

    def u_halves(n):
        far = (u + 2) % 4
        return [
            remote(acc.at[n, far, :, pl.ds(2 * i, 2)], u_half.at[n, i], u_ssem.at[n, i], u_rsem.at[n, i], u_dev(1 + 2 * i))
            for i in range(2)
        ]

    def u_fulls(n):
        return [
            remote(acc.at[n, (u + 1 + 2 * i) % 4], u_full.at[n, i], u_ssem.at[n, 2 + i], u_rsem.at[n, 2 + i], u_dev(1 + 2 * i))
            for i in range(2)
        ]

    def v_all(n):
        return [
            remote(acc.at[n, u, (v + k) % 4], v_recv.at[n, k - 1], v_ssem.at[n, k - 1], v_rsem.at[n, k - 1], v_dev(k))
            for k in range(1, 4)
        ]

    def z_all(n):
        return [
            remote(acc.at[n, u, v, (z_half + k) % 4], z_recv.at[n, k - 1], z_ssem.at[n, k - 1], z_rsem.at[n, k - 1], z_dev(2 * k))
            for k in range(1, 4)
        ]

    def to_owner(n):
        there = place(x - x % 2 + n % 2, y - y % 2 + n // 2, z, c)
        return remote(done.at[n], owned.at[quad], own_ssem.at[n], own_rsem.at[quad], there)

    def stage0(n):
        start(u_halves(n))

    def stage1(n):
        copies = u_halves(n)
        landed(copies)
        for i in range(2):
            near = (u + 1 + 2 * i) % 4
            for b in range(4):
                acc[n, near, b, pl.ds(2 * i, 2)] += u_half[n, i, b]
        start(u_fulls(n))
        sent(copies)

    def stage2(n):
        copies = u_fulls(n)
        landed(copies)
        for b in range(4):
            acc[n, u, b] += u_full[n, 0, b] + u_full[n, 1, b]
        start(v_all(n))
        sent(copies)

    def stage3(n):
        copies = v_all(n)
        landed(copies)
        acc[n, u, v] += (v_recv[n, 0] + v_recv[n, 1]) + v_recv[n, 2]
        start(z_all(n))
        sent(copies)

    def stage4(n):
        copies = z_all(n)
        landed(copies)
        total = (acc[n, u, v, z_half] + z_recv[n, 0]) + (z_recv[n, 1] + z_recv[n, 2])

        @pl.when(quad == n)
        def _():
            owned[quad] = total

        @pl.when(quad != n)
        def _():
            done[n] = total
            to_owner(n).start()

        sent(copies)

    def out_copy(n):
        cols = pl.ds(pl.multiple_of(n * 1024, 1024), 1024)
        return pltpu.make_async_copy(out.at[:, cols], attended.at[:, cols], out_sem.at[n])

    project(0)
    project(1)
    all_queries.wait()
    all_cot.wait()

    def head(n):
        part_copy(n).wait_recv()
        kv[...] = (part_own[n] + part_recv[n]).astype(BF16)
        d_kv[...] = jnp.zeros_like(d_kv)

        def half(p, _):
            attend(n, p)
            return 0

        lax.fori_loop(0, 2, half, 0)
        out_copy(n).start()
        d_kv_t[n, :, my_rows] = d_kv[...].astype(BF16).T
        start(dkv_copies(n)[:2])
        if n + 2 < KV_HEADS:
            project(n + 2)

    head(0)
    head(1)
    forward(0)
    gradient(0)
    stage0(0)
    head(2)
    forward(1)
    stage1(0)
    gradient(1)
    stage0(1)
    head(3)
    forward(2)
    stage1(1)
    stage2(0)
    gradient(2)
    stage0(2)
    forward(3)
    stage3(0)
    stage2(1)
    gradient(3)
    stage0(3)
    stage1(2)
    stage3(1)
    stage4(0)
    stage1(3)
    stage2(2)
    stage4(1)
    stage3(2)
    stage2(3)
    stage4(2)
    stage3(3)
    stage4(3)

    for q in range(4):

        @pl.when(quad != q)
        def _():
            to_owner(q).wait_send()
            remote(done.at[q], owned.at[q], own_ssem.at[q], own_rsem.at[q], sibling).wait_recv()

    for q in range(4):
        kv_grad[q * 32:(q + 1) * 32, :] = owned[q]
    for k in range(1, 8):
        remote(mine, mine, ag_send.at[k], ag_recv.at[k], z_dev(k)).wait_send()
    sent(va)
    sent(vb)
    for r in rels:
        sent(ua[r])
        sent(ub[r])
    sent(zvs)
    sent(zus)
    for copies in zzs:
        sent(copies)
    tok_all.wait_send()
    for core in range(2):
        rows = far_tok.at[my_rows]
        remote(rows, rows, far_send.at[core], far_recv.at[core], partner[core]).wait_send()
    for n in range(KV_HEADS):
        part_copy(n).wait_send()
        sent(dkv_copies(n))
        out_copy(n).wait()


def on_device(tokens, queries, weight, cotangent):
    anywhere = pl.BlockSpec(memory_space=pl.ANY)
    vmem = pltpu.VMEM
    dma = pltpu.SemaphoreType.DMA
    return pl.pallas_call(
        kernel,
        out_shape=(
            jax.ShapeDtypeStruct((SEQ, WIDTH), BF16),
            jax.ShapeDtypeStruct((128, 128), F32),
        ),
        in_specs=[anywhere] * 4,
        out_specs=(anywhere, pl.BlockSpec(memory_space=vmem)),
        scratch_shapes=[
            vmem((2 * SEQ, HALF), BF16),
            vmem((2 * SEQ, HALF // 2), BF16),
            vmem((SEQ, WIDTH), BF16),
            vmem((SEQ, WIDTH), BF16),
            vmem((SEQ, WIDTH), BF16),
            vmem((4, 4, 8, MAIN, 128), BF16),
            vmem((8, 4, 4, 128 - MAIN, 128), BF16),
            vmem((256, HALF), BF16),
            vmem((4, SEQ, 256), F32),
            vmem((4, SEQ, 256), F32),
            vmem((4, SEQ, 256), F32),
            vmem((SEQ, 256), BF16),
            vmem((SEQ, 256), F32),
            vmem((4, 256, 2 * SEQ), BF16),
            vmem((4, 256, 2 * SEQ), BF16),
            vmem((4, 4, 4, 4, 32, 128), F32),
            vmem((4, 2, 4, 2, 32, 128), F32),
            vmem((4, 2, 4, 4, 32, 128), F32),
            vmem((4, 3, 4, 32, 128), F32),
            vmem((4, 3, 32, 128), F32),
            vmem((4, 32, 128), F32),
            vmem((4, 32, 128), F32),
            dma((5,)),
            dma((2,)),
            dma((28,)),
            dma((28,)),
            dma((15,)),
            dma((15,)),
            dma((4,)),
            dma((4,)),
            dma((4, 3)),
            dma((4, 3)),
            dma((2,)),
            dma((2,)),
            dma((4, 4)),
            dma((4, 4)),
            dma((4, 3)),
            dma((4, 3)),
            dma((4, 3)),
            dma((4, 3)),
            dma((4,)),
            dma((4,)),
            dma((4,)),
        ],
        compiler_params=pltpu.CompilerParams(
            collective_id=0, has_side_effects=True, vmem_limit_bytes=56 * 2**20
        ),
        cost_estimate=pl.CostEstimate(flops=12 * 10**9, bytes_accessed=16 * 2**20, transcendentals=4 * 10**6),
    )(tokens, queries, weight, cotangent)


def solution(mesh):
    placed = (
        P(("dp", "pipe"), None),
        P(("dp", "pipe"), None),
        P("pipe", "dp"),
        P(("dp", "pipe"), None),
    )
    return jax.shard_map(
        on_device,
        mesh=mesh,
        in_specs=placed,
        out_specs=(P(("dp", "pipe"), None), P("pipe", "dp")),
        check_vma=False,
    )
```

```python
import functools
import math

import jax
import jax.numpy as jnp
from jax import lax
from jax.experimental import pallas as pl
from jax.experimental.pallas import tpu as pltpu
from jax.sharding import PartitionSpec as P

SEQ = 384
WIDTH = 4096
HALF = 2048
KV_HEADS = 4
HEAD = 128
SCALE = 1.0 / math.sqrt(HEAD)
LOG2E = math.log2(math.e)
MESH = pl.DeviceIdType.MESH
F32 = jnp.float32
BF16 = jnp.bfloat16
MAIN = 96
NT = (((1,), (1,)), ((), ()))


def place(x, y, z, c):
    return (z * 4 + (x // 2) * 2 + c, y * 2 + x % 2)


def kernel(
    tokens, queries, weight, cotangent, attended, kv_grad,
    tok, tok_t, qry, cot, out, gathered, gathered_z, head_weight, part, part_recv,
    kv, d_kv, d_kv_t, acc, u_half, u_full, v_half, v_full, z_recv, done, owned, zacc, z_half, z_full, zu_recv, zv_recv,
    load_sem, tok_sem, ag_send, ag_recv, zg_send, zg_recv, part_ssem, part_rsem, dkv_ssem, dkv_rsem, zr_send, zr_recv,
    u_ssem, u_rsem, v_ssem, v_rsem, z_ssem, z_rsem, own_ssem, own_rsem, out_sem,
):
    dp, pipe = lax.axis_index("dp"), lax.axis_index("pipe")
    c, x, y, z = dp % 2, 2 * ((dp // 2) % 2) + pipe % 2, pipe // 2, dp // 4
    u, v = x + c * (y - x), y + c * (x - y)

    def uv(a, b):
        return place(a + c * (b - a), b + c * (a - b), z, c)

    def u_dev(step):
        return uv((u + step) % 4, v)

    def v_dev(step):
        return uv(u, (v + step) % 4)

    def z_dev(step):
        return place(x, y, (z + step) % 8, c)

    sibling = place(x, y, z, 1 - c)
    quad = 2 * (y % 2) + x % 2

    def remote(src, dst, ssem, rsem, device):
        return pltpu.make_async_remote_copy(
            src_ref=src, dst_ref=dst, send_sem=ssem, recv_sem=rsem,
            device_id=device, device_id_type=MESH,
        )

    own_weight = pltpu.make_async_copy(weight.at[pl.ds(0, MAIN)], gathered.at[u, v, z], load_sem.at[0])
    own_rest = pltpu.make_async_copy(weight.at[pl.ds(MAIN, 128 - MAIN)], gathered_z.at[z, u, v], load_sem.at[4])
    own_weight.start()
    own_rest.start()

    def load_tokens(k, _):
        pltpu.make_async_copy(
            tokens.at[:, pl.ds(pl.multiple_of((2 * k + c) * 128, 128), 128)],
            tok.at[pl.ds(pl.multiple_of(c * SEQ, SEQ), SEQ), pl.ds(pl.multiple_of(k * 128, 128), 128)],
            load_sem.at[1],
        ).start()
        return 0

    lax.fori_loop(0, 16, load_tokens, 0)
    all_queries = pltpu.make_async_copy(queries, qry, load_sem.at[2])
    all_cot = pltpu.make_async_copy(cotangent, cot, load_sem.at[3])
    all_queries.start()
    all_cot.start()

    barrier = pltpu.get_barrier_semaphore()
    peers = [u_dev(k) for k in range(1, 4)] + [v_dev(k) for k in range(1, 4)] + [sibling]
    peers += [z_dev(k) for k in range(1, 8)]
    peers += [place(x + 1 - 2 * (x % 2), y + 1 - 2 * (y % 2), z, c)]
    for peer in peers:
        pl.semaphore_signal(barrier, inc=1, device_id=peer, device_id_type=MESH)
    pl.semaphore_wait(barrier, len(peers))

    own_weight.wait()
    mine = gathered.at[u, v, z]
    for k in range(1, 8):
        remote(mine, mine, ag_send.at[k], ag_recv.at[k], z_dev(k)).start()

    own_rest.wait()

    def zv(k):
        here = gathered_z.at[z, u, v]
        return remote(here, here, zg_send.at[k], zg_recv.at[k], v_dev(k))

    def zu(k):
        here = gathered_z.at[z, u]
        return remote(here, here, zg_send.at[3 + k], zg_recv.at[3 + k], u_dev(k))

    def zz(hop, way):
        here = gathered_z.at[(z - way * hop + 8) % 8]
        if hop == 3:
            here = here.at[pl.ds(0 if way == 1 else 2, 2)]
        sem = 7 + 2 * hop + (way == -1)
        return remote(here, here, zg_send.at[sem], zg_recv.at[sem], z_dev(8 + way))

    zvs = [zv(k) for k in range(1, 4)]
    zus = [zu(k) for k in range(1, 4)]
    zzs = [[zz(hop, 1), zz(hop, -1)] for hop in range(4)]
    for copy in zvs:
        copy.start()

    my_rows = pl.ds(pl.multiple_of(c * SEQ, SEQ), SEQ)
    sib_rows = pl.ds(pl.multiple_of((1 - c) * SEQ, SEQ), SEQ)

    def send_tokens(k, _):
        remote(
            tokens.at[:, pl.ds(pl.multiple_of((2 * k + 1 - c) * 128, 128), 128)],
            tok.at[my_rows, pl.ds(pl.multiple_of(k * 128, 128), 128)],
            tok_sem.at[0], tok_sem.at[1], sibling,
        ).start()
        return 0

    lax.fori_loop(0, 16, send_tokens, 0)

    def v_first(step, sem):
        row = gathered.at[u, v]
        return remote(row, row, ag_send.at[sem], ag_recv.at[sem], v_dev(step))

    def v_second(step, sem):
        row = gathered.at[u, (v - step + 4) % 4, pl.ds(0 if step == 1 else 4, 4)]
        return remote(row, row, ag_send.at[sem], ag_recv.at[sem], v_dev((step + 4) % 4))

    def u_first(step, rel, sem):
        row = gathered.at[u, (v + rel + 4) % 4]
        return remote(row, row, ag_send.at[sem], ag_recv.at[sem], u_dev((step + 4) % 4))

    def u_second(step, rel, sem):
        row = gathered.at[(u - step + 4) % 4, (v + rel + 4) % 4, pl.ds(0 if step == 1 else 4, 4)]
        return remote(row, row, ag_send.at[sem], ag_recv.at[sem], u_dev((step + 4) % 4))

    rels = (0, -1, 1, 2)
    va = [v_first(1, 8), v_first(3, 9)]
    vb = [v_second(1, 10), v_second(-1, 11)]
    ua = {r: [u_first(1, r, 12 + 2 * i), u_first(-1, r, 13 + 2 * i)] for i, r in enumerate(rels)}
    ub = {r: [u_second(1, r, 20 + 2 * i), u_second(-1, r, 21 + 2 * i)] for i, r in enumerate(rels)}

    def start(copies):
        for copy in copies:
            copy.start()

    def landed(copies):
        for copy in copies:
            copy.wait_recv()

    def sent(copies):
        for copy in copies:
            copy.wait_send()

    landed(zvs)
    start(zus)
    for k in range(1, 8):
        here = gathered.at[u, v, (z - k + 8) % 8]
        remote(mine, here, ag_send.at[k], ag_recv.at[k], z_dev(k)).wait_recv()
    start(va)
    start(ua[0])
    landed(zus)
    start(zzs[0])
    landed(va)
    start(vb)
    start(ua[-1])
    start(ua[1])
    own_tok = pltpu.make_async_copy(tok.at[my_rows], tok.at[my_rows], load_sem.at[1])
    own_tok.wait()
    tok_all = remote(tok.at[my_rows], tok.at[sib_rows], tok_sem.at[0], tok_sem.at[1], sibling)
    tok_all.wait_recv()

    def turn(i):
        tok_t[i * 256:(i + 1) * 256, :] = tok[:, i * 256:(i + 1) * 256].T

    turn(0)
    landed(zzs[0])
    start(zzs[1])
    turn(1)
    landed(ua[0])
    start(ub[0])
    landed(vb)
    start(ua[2])
    turn(2)
    turn(3)
    landed(zzs[1])
    start(zzs[2])
    landed(ua[-1])
    start(ub[-1])
    turn(4)
    landed(ua[1])
    start(ub[1])
    turn(5)
    landed(zzs[2])
    start(zzs[3])
    turn(6)
    landed(ua[2])
    start(ub[2])
    turn(7)
    for r in rels:
        landed(ub[r])
    landed(zzs[3])

    def part_copy(n):
        return remote(part.at[n, sib_rows], part_recv.at[n], part_ssem.at[n], part_rsem.at[n], sibling)

    def project(n):
        for kind in range(2):
            for x_hi in range(2):
                wx, wy = 2 * x_hi + n % 2, n // 2 + 2 * kind
                wu, wv = wx + c * (wy - wx), wy + c * (wx - wy)
                for wz in range(8):
                    k = wz * 2 + x_hi
                    cols, row = slice(k * 128, (k + 1) * 128), kind * 128
                    head_weight[row:row + MAIN, cols] = gathered[wu, wv, wz]
                    head_weight[row + MAIN:row + 128, cols] = gathered_z[wz, wu, wv]
        part[n] = lax.dot_general(tok[...], head_weight[...], NT, preferred_element_type=F32)
        part_copy(n).start()

    def attend(n, p):
        base = pl.multiple_of((n * 2 + p) * 512, 512)
        at_key = lax.broadcasted_iota(jnp.int32, (128, 512), 0)
        at_query = lax.broadcasted_iota(jnp.int32, (128, 512), 1) % 128

        def heads(ref, j):
            block = ref[j * 128:(j + 1) * 128, pl.ds(base, 512)]
            return jnp.concatenate([block[:, h * 128:(h + 1) * 128] for h in range(4)], axis=0)

        def products(j):
            q, g, span = heads(qry, j), heads(cot, j), (j + 1) * 128
            scores = lax.dot_general(kv[:span, :128], q, NT, preferred_element_type=F32)
            d_probs = lax.dot_general(kv[:span, 128:], g, NT, preferred_element_type=F32)
            return q, g, scores, d_probs

        def softmax(j, scores, d_probs):
            diagonal = jnp.where(at_key <= at_query, scores[j * 128:], -1e30)
            scores = diagonal if j == 0 else jnp.concatenate([scores[: j * 128], diagonal], axis=0)
            top = jnp.max(scores, axis=0, keepdims=True)
            grown = jnp.exp2((scores - top) * (SCALE * LOG2E))
            share_of = 1.0 / jnp.sum(grown, axis=0, keepdims=True)
            weighed = grown * d_probs
            inner = jnp.sum(weighed, axis=0, keepdims=True) * share_of
            d_scores = (weighed - grown * inner) * (share_of * SCALE)
            return (grown * share_of).astype(BF16), d_scores.astype(BF16)

        blocks = [products(j) for j in range(3)]
        halves = [softmax(j, blocks[j][2], blocks[j][3]) for j in range(3)]
        d_keys, d_values = [], []
        for j in range(3):
            q, g = blocks[j][:2]
            probs_half, d_scores = halves[j]
            seen = lax.dot_general(
                kv[: (j + 1) * 128, 128:], probs_half, (((0,), (0,)), ((), ())), preferred_element_type=F32
            ).astype(BF16)
            for h in range(4):
                out[j * 128:(j + 1) * 128, pl.ds(base + h * 128, 128)] = seen[:, h * 128:(h + 1) * 128].T
            d_keys.append(jnp.dot(d_scores, q, preferred_element_type=F32))
            d_values.append(jnp.dot(probs_half, g, preferred_element_type=F32))
        for t in range(3):
            rows = slice(t * 128, (t + 1) * 128)
            d_kv[rows, :128] += sum(d_keys[j][rows] for j in range(t, 3))
            d_kv[rows, 128:] += sum(d_values[j][rows] for j in range(t, 3))

    def dkv_copy(n):
        here = d_kv_t.at[n, my_rows]
        return remote(here, here, dkv_ssem.at[n], dkv_rsem.at[n], sibling)

    def gradient(n):
        dkv_copy(n).wait_recv()
        rhs = d_kv_t[n]

        @pl.loop(0, 2)
        def _(part_of):
            lhs = tok_t[pl.ds(pl.multiple_of(part_of * 1024, 1024), 1024), :]
            block = jnp.dot(lhs, rhs, preferred_element_type=F32)
            for step in range(4):
                gz = part_of * 4 + step
                for kind in range(2):
                    for q in range(4):
                        for x_hi in range(2):
                            gx, gy = 2 * x_hi + q % 2, 2 * kind + q // 2
                            gu, gv = gx + c * (gy - gx), gy + c * (gx - gy)
                            row = step * 256 + x_hi * 128 + q * 32
                            piece = block[row:row + 32, kind * 128:(kind + 1) * 128]
                            if n == 0:
                                zacc[gz, gu, gv] = piece
                            else:
                                acc[n, gu, (gv - v + 6) % 4, gz] = piece

    slices = (slice(0, 1), slice(1, 4))

    def u_halves(n, part):
        far, rows = (u + 2) % 4, pl.ds(part, 1 + 2 * part)
        return [
            remote(
                acc.at[n, far, rows, pl.ds(4 * i, 4)], u_half.at[n, i, rows],
                u_ssem.at[n, 4 * part + i], u_rsem.at[n, 4 * part + i], u_dev(1 + 2 * i),
            )
            for i in range(2)
        ]

    def u_fulls(n, part):
        rows = pl.ds(part, 1 + 2 * part)
        return [
            remote(
                acc.at[n, (u + 1 + 2 * i) % 4, rows], u_full.at[n, i, rows],
                u_ssem.at[n, 4 * part + 2 + i], u_rsem.at[n, 4 * part + 2 + i], u_dev(1 + 2 * i),
            )
            for i in range(2)
        ]

    def v_halves(n):
        return [
            remote(acc.at[n, u, 0, pl.ds(4 * i, 4)], v_half.at[n, i], v_ssem.at[n, i], v_rsem.at[n, i], v_dev(1 + 2 * i))
            for i in range(2)
        ]

    def v_fulls(n):
        return [
            remote(acc.at[n, u, 3 - 2 * i], v_full.at[n, i], v_ssem.at[n, 2 + i], v_rsem.at[n, 2 + i], v_dev(1 + 2 * i))
            for i in range(2)
        ]

    def z_all(n):
        return [
            remote(acc.at[n, u, 2, (z + k) % 8], z_recv.at[n, k - 1], z_ssem.at[n, k - 1], z_rsem.at[n, k - 1], z_dev(k))
            for k in range(1, 8)
        ]

    def to_owner(n):
        there = place(x - x % 2 + n % 2, y - y % 2 + n // 2, z, c)
        return remote(done.at[n], owned.at[quad], own_ssem.at[n], own_rsem.at[quad], there)

    def stage0(n):
        start(u_halves(n, 0))
        start(u_halves(n, 1))

    def stage1(n, part):
        copies = u_halves(n, part)
        landed(copies)
        for i in range(2):
            near = (u + 1 + 2 * i) % 4
            for b in range(*slices[part].indices(4)):
                acc[n, near, b, pl.ds(4 * i, 4)] += u_half[n, i, b]
        start(u_fulls(n, part))
        sent(copies)

    def stage2(n, part):
        copies = u_fulls(n, part)
        landed(copies)
        for b in range(*slices[part].indices(4)):
            acc[n, u, b] += u_full[n, 0, b] + u_full[n, 1, b]
        if part == 0:
            start(v_halves(n))
        sent(copies)

    def stage3(n):
        copies = v_halves(n)
        landed(copies)
        for i in range(2):
            acc[n, u, 3 - 2 * i, pl.ds(4 * i, 4)] += v_half[n, i]
        start(v_fulls(n))
        sent(copies)

    def stage4(n):
        copies = v_fulls(n)
        landed(copies)
        acc[n, u, 2] += v_full[n, 0] + v_full[n, 1]
        start(z_all(n))
        sent(copies)

    def hand_over(n, total):
        @pl.when(quad == n)
        def _():
            owned[quad] = total

        @pl.when(quad != n)
        def _():
            done[n] = total
            to_owner(n).start()

    def stage5(n):
        copies = z_all(n)
        landed(copies)
        total = acc[n, u, 2, z]
        for k in range(7):
            total = total + z_recv[n, k]
        hand_over(n, total)
        sent(copies)

    def ring_halves():
        far = (z + 4) % 8
        return [
            remote(zacc.at[far, pl.ds(2 * i, 2)], z_half.at[i], zr_send.at[i], zr_recv.at[i], z_dev(1 + 6 * i))
            for i in range(2)
        ]

    def ring_fulls(hop):
        return [
            remote(
                zacc.at[(z + (hop if i == 0 else 8 - hop)) % 8], z_full.at[3 - hop, i],
                zr_send.at[2 * (4 - hop) + i], zr_recv.at[2 * (4 - hop) + i], z_dev(1 + 6 * i),
            )
            for i in range(2)
        ]

    def ring_u():
        return [
            remote(zacc.at[z, (u + k) % 4], zu_recv.at[k - 1], zr_send.at[7 + k], zr_recv.at[7 + k], u_dev(k))
            for k in range(1, 4)
        ]

    def ring_v():
        return [
            remote(zacc.at[z, u, (v + k) % 4], zv_recv.at[k - 1], zr_send.at[10 + k], zr_recv.at[10 + k], v_dev(k))
            for k in range(1, 4)
        ]

    def ring0():
        start(ring_halves())

    def ring1():
        copies = ring_halves()
        landed(copies)
        for i in range(2):
            zacc[(z + 3 + 2 * i) % 8, pl.ds(2 * i, 2)] += z_half[i]
        start(ring_fulls(3))
        sent(copies)

    def ring2(hop):
        copies = ring_fulls(hop + 1)
        landed(copies)
        for i in range(2):
            near = (z + (hop if i == 0 else 8 - hop)) % 8
            for b in range(4):
                zacc[near, b] += z_full[2 - hop, i, b]
        start(ring_fulls(hop))
        sent(copies)

    def ring4():
        copies = ring_fulls(1)
        landed(copies)
        for b in range(4):
            zacc[z, b] += z_full[2, 0, b] + z_full[2, 1, b]
        start(ring_u())
        sent(copies)

    def ring5():
        copies = ring_u()
        landed(copies)
        zacc[z, u] += (zu_recv[0] + zu_recv[1]) + zu_recv[2]
        start(ring_v())
        sent(copies)

    def ring6():
        copies = ring_v()
        landed(copies)
        hand_over(0, (zacc[z, u, v] + zv_recv[0]) + (zv_recv[1] + zv_recv[2]))
        sent(copies)

    def out_copy(n):
        cols = pl.ds(pl.multiple_of(n * 1024, 1024), 1024)
        return pltpu.make_async_copy(out.at[:, cols], attended.at[:, cols], out_sem.at[n])

    project(0)
    project(1)
    all_queries.wait()
    all_cot.wait()

    def head(n):
        part_copy(n).wait_recv()
        kv[...] = (part[n, my_rows] + part_recv[n]).astype(BF16)
        d_kv[...] = jnp.zeros_like(d_kv)

        def half(p, _):
            attend(n, p)
            return 0

        lax.fori_loop(0, 2, half, 0)
        out_copy(n).start()
        d_kv_t[n, my_rows] = d_kv[...].astype(BF16)
        dkv_copy(n).start()

    head(0)
    project(2)
    gradient(0)
    ring0()
    head(1)
    ring1()
    project(3)
    gradient(1)
    stage0(1)
    head(2)
    stage1(1, 0)
    stage1(1, 1)
    ring2(2)
    gradient(2)
    stage0(2)
    head(3)
    stage1(2, 0)
    stage1(2, 1)
    gradient(3)
    stage0(3)
    stage2(1, 0)
    ring2(1)
    stage2(1, 1)
    stage1(3, 0)
    stage2(2, 0)
    stage3(1)
    stage1(3, 1)
    stage2(2, 1)
    stage3(2)
    ring4()
    stage2(3, 0)
    stage4(1)
    stage4(2)
    stage2(3, 1)
    stage3(3)
    ring5()
    stage5(1)
    stage5(2)
    stage4(3)
    ring6()
    stage5(3)

    for q in range(4):

        @pl.when(quad != q)
        def _():
            to_owner(q).wait_send()
            remote(done.at[q], owned.at[q], own_ssem.at[q], own_rsem.at[q], sibling).wait_recv()

    kv_grad[...] = jnp.concatenate([owned[q] for q in range(4)], axis=0).T
    for k in range(1, 8):
        remote(mine, mine, ag_send.at[k], ag_recv.at[k], z_dev(k)).wait_send()
    sent(va)
    sent(vb)
    for r in rels:
        sent(ua[r])
        sent(ub[r])
    sent(zvs)
    sent(zus)
    for copies in zzs:
        sent(copies)
    tok_all.wait_send()
    for n in range(KV_HEADS):
        part_copy(n).wait_send()
        dkv_copy(n).wait_send()
        out_copy(n).wait()


def on_device(tokens, queries, weight, cotangent):
    anywhere = pl.BlockSpec(memory_space=pl.ANY)
    vmem = pltpu.VMEM
    dma = pltpu.SemaphoreType.DMA
    return pl.pallas_call(
        kernel,
        out_shape=(
            jax.ShapeDtypeStruct((SEQ, WIDTH), BF16),
            jax.ShapeDtypeStruct((128, 128), F32),
        ),
        in_specs=[anywhere] * 4,
        out_specs=(anywhere, pl.BlockSpec(memory_space=vmem)),
        scratch_shapes=[
            vmem((2 * SEQ, HALF), BF16),
            vmem((HALF, 2 * SEQ), BF16),
            vmem((SEQ, WIDTH), BF16),
            vmem((SEQ, WIDTH), BF16),
            vmem((SEQ, WIDTH), BF16),
            vmem((4, 4, 8, MAIN, 128), BF16),
            vmem((8, 4, 4, 128 - MAIN, 128), BF16),
            vmem((256, HALF), BF16),
            vmem((4, 2 * SEQ, 256), F32),
            vmem((4, SEQ, 256), F32),
            vmem((SEQ, 256), BF16),
            vmem((SEQ, 256), F32),
            vmem((4, 2 * SEQ, 256), BF16),
            vmem((4, 4, 4, 8, 32, 128), F32),
            vmem((4, 2, 4, 4, 32, 128), F32),
            vmem((4, 2, 4, 8, 32, 128), F32),
            vmem((4, 2, 4, 32, 128), F32),
            vmem((4, 2, 8, 32, 128), F32),
            vmem((4, 7, 32, 128), F32),
            vmem((4, 32, 128), F32),
            vmem((4, 32, 128), F32),
            vmem((8, 4, 4, 32, 128), F32),
            vmem((2, 2, 4, 32, 128), F32),
            vmem((3, 2, 4, 4, 32, 128), F32),
            vmem((3, 4, 32, 128), F32),
            vmem((3, 32, 128), F32),
            dma((5,)),
            dma((2,)),
            dma((28,)),
            dma((28,)),
            dma((15,)),
            dma((15,)),
            dma((4,)),
            dma((4,)),
            dma((4,)),
            dma((4,)),
            dma((14,)),
            dma((14,)),
            dma((4, 8)),
            dma((4, 8)),
            dma((4, 4)),
            dma((4, 4)),
            dma((4, 7)),
            dma((4, 7)),
            dma((4,)),
            dma((4,)),
            dma((4,)),
        ],
        compiler_params=pltpu.CompilerParams(
            collective_id=0, has_side_effects=True, vmem_limit_bytes=56 * 2**20
        ),
        cost_estimate=pl.CostEstimate(flops=12 * 10**9, bytes_accessed=16 * 2**20, transcendentals=4 * 10**6),
    )(tokens, queries, weight, cotangent)


def solution(mesh):
    placed = (
        P(("dp", "pipe"), None),
        P(("dp", "pipe"), None),
        P("pipe", "dp"),
        P(("dp", "pipe"), None),
    )
    return jax.shard_map(
        on_device,
        mesh=mesh,
        in_specs=placed,
        out_specs=(P(("dp", "pipe"), None), P("pipe", "dp")),
        check_vma=False,
    )
```

```python
import functools
import math

import jax
import jax.numpy as jnp
from jax import lax
from jax.experimental import pallas as pl
from jax.experimental.pallas import tpu as pltpu
from jax.sharding import PartitionSpec as P

SEQ = 384
WIDTH = 4096
HALF = 2048
KV_HEADS = 4
HEAD = 128
SCALE = 1.0 / math.sqrt(HEAD)
LOG2E = math.log2(math.e)
MESH = pl.DeviceIdType.MESH
F32 = jnp.float32
BF16 = jnp.bfloat16
MAIN = 96
NT = (((1,), (1,)), ((), ()))


def place(x, y, z, c):
    return (z * 4 + (x // 2) * 2 + c, y * 2 + x % 2)


def kernel(
    tokens, queries, weight, cotangent, attended, kv_grad,
    tok, tok_t, qry, cot, out, gathered, gathered_z, head_weight, part, part_recv,
    kv, d_kv, d_kv_t, acc, u_half, u_full, v_half, v_full, z_recv, done, owned, zacc, z_half, z_full, zu_recv, zv_recv,
    load_sem, tok_sem, ag_send, ag_recv, zg_send, zg_recv, part_ssem, part_rsem, dkv_ssem, dkv_rsem, zr_send, zr_recv,
    u_ssem, u_rsem, v_ssem, v_rsem, z_ssem, z_rsem, own_ssem, own_rsem, out_sem,
):
    dp, pipe = lax.axis_index("dp"), lax.axis_index("pipe")
    c, x, y, z = dp % 2, 2 * ((dp // 2) % 2) + pipe % 2, pipe // 2, dp // 4
    u, v = x + c * (y - x), y + c * (x - y)

    def uv(a, b):
        return place(a + c * (b - a), b + c * (a - b), z, c)

    def u_dev(step):
        return uv((u + step) % 4, v)

    def v_dev(step):
        return uv(u, (v + step) % 4)

    def z_dev(step):
        return place(x, y, (z + step) % 8, c)

    sibling = place(x, y, z, 1 - c)
    quad = 2 * (y % 2) + x % 2

    def remote(src, dst, ssem, rsem, device):
        return pltpu.make_async_remote_copy(
            src_ref=src, dst_ref=dst, send_sem=ssem, recv_sem=rsem,
            device_id=device, device_id_type=MESH,
        )

    own_weight = pltpu.make_async_copy(weight.at[pl.ds(0, MAIN)], gathered.at[u, v, z], load_sem.at[0])
    own_rest = pltpu.make_async_copy(weight.at[pl.ds(MAIN, 128 - MAIN)], gathered_z.at[z, u, v], load_sem.at[4])
    own_weight.start()
    own_rest.start()

    def load_tokens(k, _):
        pltpu.make_async_copy(
            tokens.at[:, pl.ds(pl.multiple_of((2 * k + c) * 128, 128), 128)],
            tok.at[pl.ds(pl.multiple_of(c * SEQ, SEQ), SEQ), pl.ds(pl.multiple_of(k * 128, 128), 128)],
            load_sem.at[1],
        ).start()
        return 0

    lax.fori_loop(0, 16, load_tokens, 0)
    all_queries = pltpu.make_async_copy(queries, qry, load_sem.at[2])
    all_cot = pltpu.make_async_copy(cotangent, cot, load_sem.at[3])
    all_queries.start()
    all_cot.start()

    barrier = pltpu.get_barrier_semaphore()
    peers = [u_dev(k) for k in range(1, 4)] + [v_dev(k) for k in range(1, 4)] + [sibling]
    peers += [z_dev(k) for k in range(1, 8)]
    peers += [place(x + 1 - 2 * (x % 2), y + 1 - 2 * (y % 2), z, c)]
    for peer in peers:
        pl.semaphore_signal(barrier, inc=1, device_id=peer, device_id_type=MESH)
    pl.semaphore_wait(barrier, len(peers))

    own_weight.wait()
    mine = gathered.at[u, v, z]
    for k in range(1, 8):
        remote(mine, mine, ag_send.at[k], ag_recv.at[k], z_dev(k)).start()

    own_rest.wait()

    def zv(k):
        here = gathered_z.at[z, u, v]
        return remote(here, here, zg_send.at[k], zg_recv.at[k], v_dev(k))

    def zu(k):
        here = gathered_z.at[z, u]
        return remote(here, here, zg_send.at[3 + k], zg_recv.at[3 + k], u_dev(k))

    def zz(hop, way):
        here = gathered_z.at[(z - way * hop + 8) % 8]
        if hop == 3:
            here = here.at[pl.ds(0 if way == 1 else 2, 2)]
        sem = 7 + 2 * hop + (way == -1)
        return remote(here, here, zg_send.at[sem], zg_recv.at[sem], z_dev(8 + way))

    zvs = [zv(k) for k in range(1, 4)]
    zus = [zu(k) for k in range(1, 4)]
    zzs = [[zz(hop, 1), zz(hop, -1)] for hop in range(4)]
    for copy in zvs:
        copy.start()

    my_rows = pl.ds(pl.multiple_of(c * SEQ, SEQ), SEQ)
    sib_rows = pl.ds(pl.multiple_of((1 - c) * SEQ, SEQ), SEQ)

    def send_tokens(k, _):
        remote(
            tokens.at[:, pl.ds(pl.multiple_of((2 * k + 1 - c) * 128, 128), 128)],
            tok.at[my_rows, pl.ds(pl.multiple_of(k * 128, 128), 128)],
            tok_sem.at[0], tok_sem.at[1], sibling,
        ).start()
        return 0

    lax.fori_loop(0, 16, send_tokens, 0)

    def v_first(step, sem):
        row = gathered.at[u, v]
        return remote(row, row, ag_send.at[sem], ag_recv.at[sem], v_dev(step))

    def v_second(step, sem):
        row = gathered.at[u, (v - step + 4) % 4, pl.ds(0 if step == 1 else 4, 4)]
        return remote(row, row, ag_send.at[sem], ag_recv.at[sem], v_dev((step + 4) % 4))

    def u_first(step, rel, sem):
        row = gathered.at[u, (v + rel + 4) % 4]
        return remote(row, row, ag_send.at[sem], ag_recv.at[sem], u_dev((step + 4) % 4))

    def u_second(step, rel, sem):
        row = gathered.at[(u - step + 4) % 4, (v + rel + 4) % 4, pl.ds(0 if step == 1 else 4, 4)]
        return remote(row, row, ag_send.at[sem], ag_recv.at[sem], u_dev((step + 4) % 4))

    rels = (0, -1, 1, 2)
    va = [v_first(1, 8), v_first(3, 9)]
    vb = [v_second(1, 10), v_second(-1, 11)]
    ua = {r: [u_first(1, r, 12 + 2 * i), u_first(-1, r, 13 + 2 * i)] for i, r in enumerate(rels)}
    ub = {r: [u_second(1, r, 20 + 2 * i), u_second(-1, r, 21 + 2 * i)] for i, r in enumerate(rels)}

    def start(copies):
        for copy in copies:
            copy.start()

    def landed(copies):
        for copy in copies:
            copy.wait_recv()

    def sent(copies):
        for copy in copies:
            copy.wait_send()

    landed(zvs)
    start(zus)
    for k in range(1, 8):
        here = gathered.at[u, v, (z - k + 8) % 8]
        remote(mine, here, ag_send.at[k], ag_recv.at[k], z_dev(k)).wait_recv()
    start(va)
    start(ua[0])
    landed(zus)
    start(zzs[0])
    landed(va)
    start(vb)
    start(ua[-1])
    start(ua[1])
    own_tok = pltpu.make_async_copy(tok.at[my_rows], tok.at[my_rows], load_sem.at[1])
    own_tok.wait()
    tok_all = remote(tok.at[my_rows], tok.at[sib_rows], tok_sem.at[0], tok_sem.at[1], sibling)
    tok_all.wait_recv()

    def turn(i):
        tok_t[i * 256:(i + 1) * 256, :] = tok[:, i * 256:(i + 1) * 256].T

    turn(0)
    landed(zzs[0])
    start(zzs[1])
    turn(1)
    landed(ua[0])
    start(ub[0])
    landed(vb)
    start(ua[2])
    turn(2)
    turn(3)
    landed(zzs[1])
    start(zzs[2])
    landed(ua[-1])
    start(ub[-1])
    turn(4)
    landed(ua[1])
    start(ub[1])
    turn(5)
    landed(zzs[2])
    start(zzs[3])
    turn(6)
    landed(ua[2])
    start(ub[2])
    turn(7)
    for r in rels:
        landed(ub[r])
    landed(zzs[3])

    def part_copy(n):
        return remote(part.at[n, sib_rows], part_recv.at[n], part_ssem.at[n], part_rsem.at[n], sibling)

    def project(n):
        for kind in range(2):
            for x_hi in range(2):
                wx, wy = 2 * x_hi + n % 2, n // 2 + 2 * kind
                wu, wv = wx + c * (wy - wx), wy + c * (wx - wy)
                for wz in range(8):
                    k = wz * 2 + x_hi
                    cols, row = slice(k * 128, (k + 1) * 128), kind * 128
                    head_weight[row:row + MAIN, cols] = gathered[wu, wv, wz]
                    head_weight[row + MAIN:row + 128, cols] = gathered_z[wz, wu, wv]
        part[n] = lax.dot_general(tok[...], head_weight[...], NT, preferred_element_type=F32)
        part_copy(n).start()

    def attend(n, p):
        base = pl.multiple_of((n * 2 + p) * 512, 512)
        at_key = lax.broadcasted_iota(jnp.int32, (128, 512), 0)
        at_query = lax.broadcasted_iota(jnp.int32, (128, 512), 1) % 128

        def heads(ref, j):
            block = ref[j * 128:(j + 1) * 128, pl.ds(base, 512)]
            return jnp.concatenate([block[:, h * 128:(h + 1) * 128] for h in range(4)], axis=0)

        def products(j):
            q, g, span = heads(qry, j), heads(cot, j), (j + 1) * 128
            scores = lax.dot_general(kv[:span, :128], q, NT, preferred_element_type=F32)
            d_probs = lax.dot_general(kv[:span, 128:], g, NT, preferred_element_type=F32)
            return q, g, scores, d_probs

        def softmax(j, scores, d_probs):
            diagonal = jnp.where(at_key <= at_query, scores[j * 128:], -1e30)
            scores = diagonal if j == 0 else jnp.concatenate([scores[: j * 128], diagonal], axis=0)
            top = jnp.max(scores, axis=0, keepdims=True)
            grown = jnp.exp2((scores - top) * (SCALE * LOG2E))
            share_of = 1.0 / jnp.sum(grown, axis=0, keepdims=True)
            weighed = grown * d_probs
            inner = jnp.sum(weighed, axis=0, keepdims=True) * share_of
            d_scores = (weighed - grown * inner) * (share_of * SCALE)
            return (grown * share_of).astype(BF16), d_scores.astype(BF16)

        blocks = [products(j) for j in range(3)]
        halves = [softmax(j, blocks[j][2], blocks[j][3]) for j in range(3)]
        d_keys, d_values = [], []
        for j in range(3):
            q, g = blocks[j][:2]
            probs_half, d_scores = halves[j]
            seen = lax.dot_general(
                kv[: (j + 1) * 128, 128:], probs_half, (((0,), (0,)), ((), ())), preferred_element_type=F32
            ).astype(BF16)
            for h in range(4):
                out[j * 128:(j + 1) * 128, pl.ds(base + h * 128, 128)] = seen[:, h * 128:(h + 1) * 128].T
            d_keys.append(jnp.dot(d_scores, q, preferred_element_type=F32))
            d_values.append(jnp.dot(probs_half, g, preferred_element_type=F32))
        for t in range(3):
            rows = slice(t * 128, (t + 1) * 128)
            d_kv[rows, :128] += sum(d_keys[j][rows] for j in range(t, 3))
            d_kv[rows, 128:] += sum(d_values[j][rows] for j in range(t, 3))

    def dkv_copy(n):
        here = d_kv_t.at[n, my_rows]
        return remote(here, here, dkv_ssem.at[n], dkv_rsem.at[n], sibling)

    def gradient(n):
        dkv_copy(n).wait_recv()
        rhs = d_kv_t[n]

        @pl.loop(0, 2)
        def _(part_of):
            lhs = tok_t[pl.ds(pl.multiple_of(part_of * 1024, 1024), 1024), :]
            block = jnp.dot(lhs, rhs, preferred_element_type=F32)
            for step in range(4):
                gz = part_of * 4 + step
                for kind in range(2):
                    for q in range(4):
                        for x_hi in range(2):
                            gx, gy = 2 * x_hi + q % 2, 2 * kind + q // 2
                            gu, gv = gx + c * (gy - gx), gy + c * (gx - gy)
                            row = step * 256 + x_hi * 128 + q * 32
                            piece = block[row:row + 32, kind * 128:(kind + 1) * 128]
                            if n == 1:
                                zacc[gz, gu, gv] = piece
                            else:
                                acc[n, gu, (gv - v + 6) % 4, gz] = piece

    slices = (slice(0, 1), slice(1, 4))

    def u_halves(n, part):
        far, rows = (u + 2) % 4, pl.ds(part, 1 + 2 * part)
        return [
            remote(
                acc.at[n, far, rows, pl.ds(4 * i, 4)], u_half.at[n, i, rows],
                u_ssem.at[n, 4 * part + i], u_rsem.at[n, 4 * part + i], u_dev(1 + 2 * i),
            )
            for i in range(2)
        ]

    def u_fulls(n, part):
        rows = pl.ds(part, 1 + 2 * part)
        return [
            remote(
                acc.at[n, (u + 1 + 2 * i) % 4, rows], u_full.at[n, i, rows],
                u_ssem.at[n, 4 * part + 2 + i], u_rsem.at[n, 4 * part + 2 + i], u_dev(1 + 2 * i),
            )
            for i in range(2)
        ]

    def v_halves(n):
        return [
            remote(acc.at[n, u, 0, pl.ds(4 * i, 4)], v_half.at[n, i], v_ssem.at[n, i], v_rsem.at[n, i], v_dev(1 + 2 * i))
            for i in range(2)
        ]

    def v_fulls(n):
        return [
            remote(acc.at[n, u, 3 - 2 * i], v_full.at[n, i], v_ssem.at[n, 2 + i], v_rsem.at[n, 2 + i], v_dev(1 + 2 * i))
            for i in range(2)
        ]

    def z_all(n):
        return [
            remote(acc.at[n, u, 2, (z + k) % 8], z_recv.at[n, k - 1], z_ssem.at[n, k - 1], z_rsem.at[n, k - 1], z_dev(k))
            for k in range(1, 8)
        ]

    def to_owner(n):
        there = place(x - x % 2 + n % 2, y - y % 2 + n // 2, z, c)
        return remote(done.at[n], owned.at[quad], own_ssem.at[n], own_rsem.at[quad], there)

    def stage0(n):
        start(u_halves(n, 0))
        start(u_halves(n, 1))

    def stage1(n, part):
        copies = u_halves(n, part)
        landed(copies)
        for i in range(2):
            near = (u + 1 + 2 * i) % 4
            for b in range(*slices[part].indices(4)):
                acc[n, near, b, pl.ds(4 * i, 4)] += u_half[n, i, b]
        start(u_fulls(n, part))
        sent(copies)

    def stage2(n, part):
        copies = u_fulls(n, part)
        landed(copies)
        for b in range(*slices[part].indices(4)):
            acc[n, u, b] += u_full[n, 0, b] + u_full[n, 1, b]
        if part == 0:
            start(v_halves(n))
        sent(copies)

    def stage3(n):
        copies = v_halves(n)
        landed(copies)
        for i in range(2):
            acc[n, u, 3 - 2 * i, pl.ds(4 * i, 4)] += v_half[n, i]
        start(v_fulls(n))
        sent(copies)

    def stage4(n):
        copies = v_fulls(n)
        landed(copies)
        acc[n, u, 2] += v_full[n, 0] + v_full[n, 1]
        start(z_all(n))
        sent(copies)

    def hand_over(n, total):
        @pl.when(quad == n)
        def _():
            owned[quad] = total

        @pl.when(quad != n)
        def _():
            done[n] = total
            to_owner(n).start()

    def stage5(n):
        copies = z_all(n)
        landed(copies)
        total = acc[n, u, 2, z]
        for k in range(7):
            total = total + z_recv[n, k]
        hand_over(n, total)
        sent(copies)

    def ring_halves():
        far = (z + 4) % 8
        return [
            remote(zacc.at[far, pl.ds(2 * i, 2)], z_half.at[i], zr_send.at[i], zr_recv.at[i], z_dev(1 + 6 * i))
            for i in range(2)
        ]

    def ring_fulls(hop):
        return [
            remote(
                zacc.at[(z + (hop if i == 0 else 8 - hop)) % 8], z_full.at[3 - hop, i],
                zr_send.at[2 * (4 - hop) + i], zr_recv.at[2 * (4 - hop) + i], z_dev(1 + 6 * i),
            )
            for i in range(2)
        ]

    def ring_u():
        return [
            remote(zacc.at[z, (u + k) % 4], zu_recv.at[k - 1], zr_send.at[7 + k], zr_recv.at[7 + k], u_dev(k))
            for k in range(1, 4)
        ]

    def ring_v():
        return [
            remote(zacc.at[z, u, (v + k) % 4], zv_recv.at[k - 1], zr_send.at[10 + k], zr_recv.at[10 + k], v_dev(k))
            for k in range(1, 4)
        ]

    def ring0():
        start(ring_halves())

    def ring1():
        copies = ring_halves()
        landed(copies)
        for i in range(2):
            zacc[(z + 3 + 2 * i) % 8, pl.ds(2 * i, 2)] += z_half[i]
        start(ring_fulls(3))
        sent(copies)

    def ring2(hop):
        copies = ring_fulls(hop + 1)
        landed(copies)
        for i in range(2):
            near = (z + (hop if i == 0 else 8 - hop)) % 8
            for b in range(4):
                zacc[near, b] += z_full[2 - hop, i, b]
        start(ring_fulls(hop))
        sent(copies)

    def ring4():
        copies = ring_fulls(1)
        landed(copies)
        for b in range(4):
            zacc[z, b] += z_full[2, 0, b] + z_full[2, 1, b]
        start(ring_u())
        sent(copies)

    def ring5():
        copies = ring_u()
        landed(copies)
        zacc[z, u] += (zu_recv[0] + zu_recv[1]) + zu_recv[2]
        start(ring_v())
        sent(copies)

    def ring6():
        copies = ring_v()
        landed(copies)
        hand_over(1, (zacc[z, u, v] + zv_recv[0]) + (zv_recv[1] + zv_recv[2]))
        sent(copies)

    def out_copy(n):
        cols = pl.ds(pl.multiple_of(n * 1024, 1024), 1024)
        return pltpu.make_async_copy(out.at[:, cols], attended.at[:, cols], out_sem.at[n])

    project(0)
    project(1)
    all_queries.wait()
    all_cot.wait()

    def head(n):
        part_copy(n).wait_recv()
        kv[...] = (part[n, my_rows] + part_recv[n]).astype(BF16)
        d_kv[...] = jnp.zeros_like(d_kv)

        def half(p, _):
            attend(n, p)
            return 0

        lax.fori_loop(0, 2, half, 0)
        out_copy(n).start()
        d_kv_t[n, my_rows] = d_kv[...].astype(BF16)
        dkv_copy(n).start()

    head(0)
    gradient(0)
    stage0(0)
    project(2)
    head(1)
    stage1(0, 0)
    stage1(0, 1)
    gradient(1)
    ring0()
    project(3)
    head(2)
    ring1()
    stage2(0, 0)
    stage2(0, 1)
    gradient(2)
    stage0(2)
    stage3(0)
    head(3)
    stage4(0)
    stage1(2, 0)
    stage1(2, 1)
    gradient(3)
    stage0(3)
    ring2(2)
    stage5(0)
    stage1(3, 0)
    stage2(2, 0)
    stage1(3, 1)
    stage2(2, 1)
    stage3(2)
    ring2(1)
    stage2(3, 0)
    stage4(2)
    stage2(3, 1)
    stage3(3)
    ring4()
    stage5(2)
    ring5()
    stage4(3)
    ring6()
    stage5(3)

    for q in range(4):

        @pl.when(quad != q)
        def _():
            to_owner(q).wait_send()
            remote(done.at[q], owned.at[q], own_ssem.at[q], own_rsem.at[q], sibling).wait_recv()

    kv_grad[...] = jnp.concatenate([owned[q] for q in range(4)], axis=0).T
    for k in range(1, 8):
        remote(mine, mine, ag_send.at[k], ag_recv.at[k], z_dev(k)).wait_send()
    sent(va)
    sent(vb)
    for r in rels:
        sent(ua[r])
        sent(ub[r])
    sent(zvs)
    sent(zus)
    for copies in zzs:
        sent(copies)
    tok_all.wait_send()
    for n in range(KV_HEADS):
        part_copy(n).wait_send()
        dkv_copy(n).wait_send()
        out_copy(n).wait()


def on_device(tokens, queries, weight, cotangent):
    anywhere = pl.BlockSpec(memory_space=pl.ANY)
    vmem = pltpu.VMEM
    dma = pltpu.SemaphoreType.DMA
    return pl.pallas_call(
        kernel,
        out_shape=(
            jax.ShapeDtypeStruct((SEQ, WIDTH), BF16),
            jax.ShapeDtypeStruct((128, 128), F32),
        ),
        in_specs=[anywhere] * 4,
        out_specs=(anywhere, pl.BlockSpec(memory_space=vmem)),
        scratch_shapes=[
            vmem((2 * SEQ, HALF), BF16),
            vmem((HALF, 2 * SEQ), BF16),
            vmem((SEQ, WIDTH), BF16),
            vmem((SEQ, WIDTH), BF16),
            vmem((SEQ, WIDTH), BF16),
            vmem((4, 4, 8, MAIN, 128), BF16),
            vmem((8, 4, 4, 128 - MAIN, 128), BF16),
            vmem((256, HALF), BF16),
            vmem((4, 2 * SEQ, 256), F32),
            vmem((4, SEQ, 256), F32),
            vmem((SEQ, 256), BF16),
            vmem((SEQ, 256), F32),
            vmem((4, 2 * SEQ, 256), BF16),
            vmem((4, 4, 4, 8, 32, 128), F32),
            vmem((4, 2, 4, 4, 32, 128), F32),
            vmem((4, 2, 4, 8, 32, 128), F32),
            vmem((4, 2, 4, 32, 128), F32),
            vmem((4, 2, 8, 32, 128), F32),
            vmem((4, 7, 32, 128), F32),
            vmem((4, 32, 128), F32),
            vmem((4, 32, 128), F32),
            vmem((8, 4, 4, 32, 128), F32),
            vmem((2, 2, 4, 32, 128), F32),
            vmem((3, 2, 4, 4, 32, 128), F32),
            vmem((3, 4, 32, 128), F32),
            vmem((3, 32, 128), F32),
            dma((5,)),
            dma((2,)),
            dma((28,)),
            dma((28,)),
            dma((15,)),
            dma((15,)),
            dma((4,)),
            dma((4,)),
            dma((4,)),
            dma((4,)),
            dma((14,)),
            dma((14,)),
            dma((4, 8)),
            dma((4, 8)),
            dma((4, 4)),
            dma((4, 4)),
            dma((4, 7)),
            dma((4, 7)),
            dma((4,)),
            dma((4,)),
            dma((4,)),
        ],
        compiler_params=pltpu.CompilerParams(
            collective_id=0, has_side_effects=True, vmem_limit_bytes=56 * 2**20
        ),
        cost_estimate=pl.CostEstimate(flops=12 * 10**9, bytes_accessed=16 * 2**20, transcendentals=4 * 10**6),
    )(tokens, queries, weight, cotangent)


def solution(mesh):
    placed = (
        P(("dp", "pipe"), None),
        P(("dp", "pipe"), None),
        P("pipe", "dp"),
        P(("dp", "pipe"), None),
    )
    return jax.shard_map(
        on_device,
        mesh=mesh,
        in_specs=placed,
        out_specs=(P(("dp", "pipe"), None), P("pipe", "dp")),
        check_vma=False,
    )
```
